256 devices in a mesh: fsdp: 32 (over x, z_lo, core), tp: 8 (over y, z_hi).
Axes of the slice: x: 4, y: 4, z: 8 (z_hi: 2, z_lo: 4; z = z_hi * 4 + z_lo), core: 2. Of those that a mesh axis runs over, the one named last changes fastest.
Arguments:
- hidden_in: bfloat16 [32768, 5120], P('fsdp', 'tp'), may hold values from -6 to 6
- out_grad: bfloat16 [32768, 5120], P('fsdp', 'tp'), may hold values from -36 to 36
- rewards: float32 [64], P('fsdp'), may hold values from -5 to 5
- group_ids: int32 [64], replicated, may hold values from 0 to 7, as said below
- weight: bfloat16 [5120, 5120], P('fsdp', 'tp'), may hold values from -0.078125 to 0.078125
- adam_m: float32 [5120, 5120], P('fsdp', 'tp'), may hold values from -6 to 6
- adam_v: float32 [5120, 5120], P('fsdp', 'tp'), may hold values from 0.05 to 2
- given_queries: bfloat16 [512, 4, 5120], P('fsdp', None, 'tp'), may hold values from -24 to 24
- given_keys: bfloat16 [512, 4, 1024], P('fsdp', None, 'tp'), may hold values from -4 to 4
- given_values: bfloat16 [512, 4, 1024], P('fsdp', None, 'tp'), may hold values from -12 to 12
- stored_keys: bfloat16 [512, 8, 512, 128], P('fsdp', 'tp'), may hold values from -24 to 24
- stored_values: bfloat16 [512, 8, 512, 128], P('fsdp', 'tp'), may hold values from -12 to 12
- cache_fill_length: int32 [512], P('fsdp'), may hold values from 128 to 508
Outputs:
- new_weight: bfloat16 [5120, 5120], P('fsdp', 'tp')
- new_m: float32 [5120, 5120], P('fsdp', 'tp')
- new_v: float32 [5120, 5120], P('fsdp', 'tp')
- layer_out: float32 [512, 4, 5120], P('fsdp', None, 'tp')
The draws below stay inside these ranges and needn't reach their ends.
Inputs may be any that keep to these rules, and one draw needn't show every extreme that they name: `group_ids`: each group number names exactly 8 sequences.
All inputs are finite; a program needn't handle non-finite values.
Results may differ from the reference program's by a relative error of at most 0.0059.
Values may be sent and summed in bfloat16 or wider, within the bound.
No kernel may reach another device: no remote copies, remote signals or barrier semaphores. Data moves between devices by JAX's collectives and lax.ppermute only.
A program may use at most 128 MiB of HBM per device.

```python
import math
import jax
import jax.numpy as jnp
from jax import lax

D = 5120
QUERY_HEADS = 40
KEY_VALUE_HEADS = 8
HEAD_SIZE = 128
QUERY_FEATURES = 5120
SEQ_LEN = 512
TOK_DEV = 1024
SEQS = 64
TOKENS = 32768
GSIZE = 8
GROUPS = 8
REPLICA_ROWS = 16
TOTAL_ROWS = 512
CACHE_SLOTS = 512
GIVEN_TOKENS = 4
OPT_STEP = 10
N_FSDP = 32


def draw_stored_keys(key, part):
    key = jax.random.fold_in(key, 1)
    value_rows = jnp.clip(jax.random.normal(key, (TOTAL_ROWS, KEY_VALUE_HEADS, CACHE_SLOTS, HEAD_SIZE), jnp.float32), -4.0, 4.0)
    return value_rows.astype(jnp.bfloat16)


def draw_given_queries(key, part):
    key = jax.random.fold_in(key, 2)
    value_rows = jnp.clip(jax.random.normal(key, (TOTAL_ROWS, GIVEN_TOKENS, QUERY_HEADS * HEAD_SIZE), jnp.float32), -4.0, 4.0)
    return value_rows.astype(jnp.bfloat16)


def draw_cache_fill_length(key, part):
    key = jax.random.fold_in(key, 3)
    lengths = jax.random.randint(key, (TOTAL_ROWS,), CACHE_SLOTS // 4, CACHE_SLOTS - GIVEN_TOKENS + 1, dtype=jnp.int32)
    lengths = lengths.at[0].set(CACHE_SLOTS - GIVEN_TOKENS)
    lengths = lengths.at[1].set(CACHE_SLOTS // 4)
    return lengths


def draw_group_ids(key, part):
    key = jax.random.fold_in(key, 4)
    order = jax.random.permutation(key, SEQS)
    return (order // GSIZE).astype(jnp.int32)


def strengthened(drawn, rng, source, target, blocks, factor):
    def block_of(dim):
        return (jnp.arange(drawn.shape[dim]) // (drawn.shape[dim] // blocks)).reshape((-1,) + (1,) * (drawn.ndim - 1 - dim))

    one_side = jax.random.permutation(rng, blocks)[block_of(target)]
    other_side = (block_of(target) + blocks // 2) % blocks
    return jnp.where((block_of(source) == one_side) | (block_of(source) == other_side), factor * drawn, drawn)


def shard_levels(key, dims, shards, low, high):
    level, own = 1.0, jax.random.fold_in(key, 6)
    for axis_at, shards_of in shards:
        draws = jnp.exp(jax.random.uniform(jax.random.fold_in(own, axis_at), (shards_of,), jnp.float32, low / len(shards), high / len(shards)))
        level = level * jnp.repeat(draws, dims[axis_at] // shards_of).reshape([-1 if axis == axis_at else 1 for axis in range(len(dims))])
    return level


def centred(own_key, dims, scale, limit, cuts=(), kind=jnp.bfloat16):
    level = shard_levels(own_key, dims, cuts, -0.22, 0.18) if cuts else 1.0
    array = jax.random.normal(own_key, dims, jnp.float32) * scale * level
    return jnp.minimum(jnp.maximum(array, -limit), limit).astype(kind)


def noise_with(stream_key, extent, scale, bound, cuts, heavy, kind=jnp.bfloat16):
    values = scale * jax.random.normal(stream_key, extent, jnp.float32)
    if cuts:
        values = values * shard_levels(stream_key, extent, cuts, -0.22, 0.18)
    return jnp.clip(strengthened(values, jax.random.fold_in(stream_key, 3), *heavy), -bound, bound).astype(kind)


def setup_inputs(seed: int = 0) -> dict:
    key_list = jax.random.split(jax.random.key(seed), 14)
    return {
        "hidden_in": centred(key_list[0], (TOKENS, QUERY_FEATURES), 1.0, 6.0, ((0, 32), (1, 8))),
        "out_grad": noise_with(key_list[1], (TOKENS, D), 6.0, 36.0, ((0, 32), (1, 8)), (0, 1, 32, 2.75)),
        "rewards": centred(key_list[2], (SEQS,), 1.0, 5.0, ((0, 32),), jnp.float32),
        "group_ids": draw_group_ids(jax.random.fold_in(key_list[13], 71), 0),
        "weight": centred(key_list[4], (D, QUERY_FEATURES), QUERY_FEATURES ** -0.5, 0.078125, ((0, 32), (1, 8))),
        "adam_m": centred(key_list[5], (D, QUERY_FEATURES), 1.0, 6.0, ((0, 32), (1, 8)), jnp.float32),
        "adam_v": jnp.clip(jnp.exp(math.log(2.0) - 3.6888794 * jax.random.uniform(key_list[6], (D, QUERY_FEATURES), jnp.float32) ** shard_levels(key_list[6], (D, QUERY_FEATURES), ((0, 32), (1, 8)), -0.2, 0.2)), 0.05, 2.0),
        "given_queries": draw_given_queries(jax.random.fold_in(key_list[13], 71), 0),
        "given_keys": centred(key_list[8], (TOTAL_ROWS, GIVEN_TOKENS, KEY_VALUE_HEADS * HEAD_SIZE), 1.0, 4.0, ((0, 32), (2, 8))),
        "given_values": centred(key_list[9], (TOTAL_ROWS, GIVEN_TOKENS, KEY_VALUE_HEADS * HEAD_SIZE), 3.0, 12.0, ((0, 32), (2, 8))),
        "stored_keys": draw_stored_keys(jax.random.fold_in(key_list[13], 71), 0),
        "stored_values": centred(key_list[11], (TOTAL_ROWS, KEY_VALUE_HEADS, CACHE_SLOTS, HEAD_SIZE), 3.0, 12.0, ((0, 32), (1, 8))),
        "cache_fill_length": draw_cache_fill_length(jax.random.fold_in(key_list[13], 71), 0),
    }


beta_one = 0.9
beta_two = 0.95
adam_eps = 1e-08
learn_rate = 0.002
decay_rate = 0.1
std_floor = 0.75

def group_advantage(rewards, group_ids):
    labels = jnp.arange(GROUPS, dtype=jnp.int32)
    member = (group_ids[:, None] == labels[None, :]).astype(jnp.float32)
    group_mean = lax.optimization_barrier(jnp.sum(member * rewards[:, None], axis=0)) / GSIZE
    spread = rewards - lax.optimization_barrier(jnp.sum(member * group_mean[None, :], axis=1))
    group_var = lax.optimization_barrier(jnp.sum(member * (spread * spread)[:, None], axis=0)) / (GSIZE - 1)
    own_std = jnp.sqrt(lax.optimization_barrier(jnp.sum(member * group_var[None, :], axis=1)))
    return spread / jnp.maximum(own_std, std_floor)

def attend_block(query_in, key_new, value_new, key_cache, value_cache, lengths):
    row_count = query_in.shape[0]
    step_count = query_in.shape[1]
    kv_heads = key_cache.shape[1]
    cache_size = key_cache.shape[2]
    head_dim = key_cache.shape[3]
    group_size = query_in.shape[2] // (kv_heads * head_dim)
    scaling = 1.0 / math.sqrt(head_dim)
    query_heads = query_in.reshape(row_count, step_count, kv_heads, group_size, head_dim).astype(jnp.float32)
    fresh_keys = key_new.reshape(row_count, step_count, kv_heads, head_dim).astype(jnp.float32)
    fresh_values = value_new.reshape(row_count, step_count, kv_heads, head_dim).astype(jnp.float32)
    cache_score = jnp.einsum('rsKgd,rKcd->rKgsc', query_heads, key_cache.astype(jnp.float32)) * scaling
    fresh_score = jnp.einsum('rsKgd,rtKd->rKgst', query_heads, fresh_keys) * scaling
    cache_mask = jnp.arange(cache_size, dtype=jnp.int32)[None, :] < lengths[:, None]
    step_index = jnp.arange(step_count, dtype=jnp.int32)
    fresh_mask = step_index[None, :] <= step_index[:, None]
    cache_score = jnp.where(cache_mask[:, None, None, None, :], cache_score, -jnp.inf)
    fresh_score = jnp.where(fresh_mask, fresh_score, -jnp.inf)
    peak_score = jnp.maximum(lax.optimization_barrier(jnp.max(cache_score, axis=-1, keepdims=True)), lax.optimization_barrier(jnp.max(fresh_score, axis=-1, keepdims=True)))
    cache_exp = jnp.exp(cache_score - peak_score)
    fresh_exp = jnp.exp(fresh_score - peak_score)
    total_exp = lax.optimization_barrier(jnp.sum(cache_exp, axis=-1, keepdims=True)) + lax.optimization_barrier(jnp.sum(fresh_exp, axis=-1, keepdims=True))
    cache_prob = (cache_exp / total_exp).astype(jnp.bfloat16)
    fresh_prob = (fresh_exp / total_exp).astype(jnp.bfloat16)
    mixed = jnp.einsum('rKgsc,rKcd->rsKgd', cache_prob.astype(jnp.float32), value_cache.astype(jnp.float32))
    mixed = mixed + jnp.einsum('rKgst,rtKd->rsKgd', fresh_prob.astype(jnp.float32), fresh_values)
    return mixed.reshape(row_count, step_count, kv_heads * group_size * head_dim).astype(jnp.bfloat16)

def reference(hidden_in, out_grad, rewards, group_ids, weight, adam_m, adam_v, given_queries, given_keys, given_values, stored_keys, stored_values, cache_fill_length):
    advantage = group_advantage(rewards, group_ids)
    token_adv = jnp.repeat(advantage, SEQ_LEN)
    weighted = (hidden_in.astype(jnp.float32) * token_adv[:, None] / SEQS).astype(jnp.bfloat16)

    def accumulate(total, index):
        start = (index * TOK_DEV).astype(jnp.int32)
        cot_rows = lax.dynamic_slice_in_dim(out_grad, start, TOK_DEV, 0).astype(jnp.float32)
        act_rows = lax.dynamic_slice_in_dim(weighted, start, TOK_DEV, 0).astype(jnp.float32)
        partial_sum = jnp.dot(cot_rows.T, act_rows, preferred_element_type=jnp.float32)
        return (total + partial_sum, None)
    gradient, _ = lax.scan(accumulate, jnp.zeros((D, QUERY_FEATURES), jnp.float32), jnp.arange(N_FSDP, dtype=jnp.int32))
    new_m = beta_one * adam_m + (1.0 - beta_one) * gradient
    new_v = beta_two * adam_v + (1.0 - beta_two) * gradient * gradient
    correct_one = 1.0 - beta_one ** OPT_STEP
    correct_two = 1.0 - beta_two ** OPT_STEP
    update = new_m / correct_one / (jnp.sqrt(new_v / correct_two) + adam_eps)
    new_weight = (weight.astype(jnp.float32) * (1.0 - learn_rate * decay_rate) - learn_rate * update).astype(jnp.bfloat16)

    def replica(inputs):
        return attend_block(*inputs)
    block_list = (given_queries.reshape(N_FSDP, REPLICA_ROWS, GIVEN_TOKENS, QUERY_FEATURES), given_keys.reshape(N_FSDP, REPLICA_ROWS, GIVEN_TOKENS, KEY_VALUE_HEADS * HEAD_SIZE), given_values.reshape(N_FSDP, REPLICA_ROWS, GIVEN_TOKENS, KEY_VALUE_HEADS * HEAD_SIZE), stored_keys.reshape(N_FSDP, REPLICA_ROWS, KEY_VALUE_HEADS, CACHE_SLOTS, HEAD_SIZE), stored_values.reshape(N_FSDP, REPLICA_ROWS, KEY_VALUE_HEADS, CACHE_SLOTS, HEAD_SIZE), cache_fill_length.reshape(N_FSDP, REPLICA_ROWS))
    attn = lax.map(replica, block_list).reshape(TOTAL_ROWS * GIVEN_TOKENS, QUERY_FEATURES)
    projected = jnp.dot(attn.astype(jnp.float32), new_weight.astype(jnp.float32).T, preferred_element_type=jnp.float32)
    layer_out = projected.reshape(TOTAL_ROWS, GIVEN_TOKENS, D)
    return (new_weight, new_m, new_v, layer_out)
```

```python
import math

import jax
import jax.numpy as jnp
from jax import lax
from jax.sharding import PartitionSpec as P

GSIZE = 8
OPT_STEP = 10

beta_one = 0.9
beta_two = 0.95
adam_eps = 1e-08
learn_rate = 0.002
decay_rate = 0.1
std_floor = 0.75

NX, ZL, CORES, NY, ZH = 4, 4, 2, 4, 2


def send(value, dest):
    pairs = []
    for x in range(NX):
        for zl in range(ZL):
            for c in range(CORES):
                for y in range(NY):
                    for zh in range(ZH):
                        to = dest(x, zl, c, y, zh)
                        pairs.append((flat(x, zl, c, y, zh), flat(*to)))
    return lax.ppermute(value, ("fsdp", "tp"), pairs)


def flat(x, zl, c, y, zh):
    return ((x * ZL + zl) * CORES + c) * (NY * ZH) + y * ZH + zh


def other_core(value):
    return send(value, lambda x, zl, c, y, zh: (x, zl, 1 - c, y, zh))


def attend_local(query_in, key_new, value_new, key_cache, value_cache, lengths):
    row_count = query_in.shape[0]
    step_count = query_in.shape[1]
    kv_heads = key_cache.shape[1]
    cache_size = key_cache.shape[2]
    head_dim = key_cache.shape[3]
    group_size = query_in.shape[2] // (kv_heads * head_dim)
    scaling = 1.0 / math.sqrt(head_dim)
    query_heads = query_in.reshape(row_count, step_count, kv_heads, group_size, head_dim)
    fresh_keys = key_new.reshape(row_count, step_count, kv_heads, head_dim)
    fresh_values = value_new.reshape(row_count, step_count, kv_heads, head_dim)
    cache_score = (
        jnp.einsum("rsKgd,rKcd->rKgsc", query_heads, key_cache, preferred_element_type=jnp.float32)
        * scaling
    )
    fresh_score = (
        jnp.einsum("rsKgd,rtKd->rKgst", query_heads, fresh_keys, preferred_element_type=jnp.float32)
        * scaling
    )
    cache_mask = jnp.arange(cache_size, dtype=jnp.int32)[None, :] < lengths[:, None]
    step_index = jnp.arange(step_count, dtype=jnp.int32)
    fresh_mask = step_index[None, :] <= step_index[:, None]
    cache_score = jnp.where(cache_mask[:, None, None, None, :], cache_score, -jnp.inf)
    fresh_score = jnp.where(fresh_mask, fresh_score, -jnp.inf)
    peak_score = jnp.maximum(
        jnp.max(cache_score, axis=-1, keepdims=True), jnp.max(fresh_score, axis=-1, keepdims=True)
    )
    cache_exp = jnp.exp(cache_score - peak_score)
    fresh_exp = jnp.exp(fresh_score - peak_score)
    total_exp = jnp.sum(cache_exp, axis=-1, keepdims=True) + jnp.sum(
        fresh_exp, axis=-1, keepdims=True
    )
    cache_prob = (cache_exp / total_exp).astype(jnp.bfloat16)
    fresh_prob = (fresh_exp / total_exp).astype(jnp.bfloat16)
    mixed = jnp.einsum(
        "rKgsc,rKcd->rsKgd", cache_prob, value_cache, preferred_element_type=jnp.float32
    )
    mixed = mixed + jnp.einsum(
        "rKgst,rtKd->rsKgd", fresh_prob, fresh_values, preferred_element_type=jnp.float32
    )
    return mixed.reshape(row_count, step_count, kv_heads * group_size * head_dim).astype(
        jnp.bfloat16
    )


def chip_advantage(rewards, group_ids, position, core):
    seq_dev = rewards.shape[0]
    devices = lax.axis_size("fsdp")
    group_count = seq_dev * devices // GSIZE
    tile = jnp.zeros((8, 128), jnp.float32).at[0, :seq_dev].set(rewards)
    tiles = lax.all_gather(tile, "fsdp", axis=0)
    every_reward = tiles[:, 0, :seq_dev].reshape(-1)
    labels = jnp.arange(group_count, dtype=jnp.int32)
    member = (group_ids[:, None] == labels[None, :]).astype(jnp.float32)
    group_mean = jnp.sum(member * every_reward[:, None], axis=0) / GSIZE
    spread = every_reward - jnp.sum(member * group_mean[None, :], axis=1)
    group_var = jnp.sum(member * (spread * spread)[:, None], axis=0) / (GSIZE - 1)
    own_std = jnp.sqrt(jnp.sum(member * group_var[None, :], axis=1))
    advantage = spread / jnp.maximum(own_std, std_floor)
    mine = lax.dynamic_slice_in_dim(advantage, position * seq_dev, seq_dev)
    theirs = lax.dynamic_slice_in_dim(advantage, (position + 1 - 2 * core) * seq_dev, seq_dev)
    return mine, theirs


def per_device(
    hidden_in,
    out_grad,
    rewards,
    group_ids,
    weight,
    adam_m,
    adam_v,
    given_queries,
    given_keys,
    given_values,
    stored_keys,
    stored_values,
    cache_fill_length,
):
    position = lax.axis_index("fsdp")
    tp_at = lax.axis_index("tp")
    x, zl, core = position // (ZL * CORES), (position // CORES) % ZL, position % CORES
    y, zh = tp_at // ZH, tp_at % ZH
    tokens, width = hidden_in.shape
    rows = weight.shape[0]
    seqs = rewards.shape[0] * lax.axis_size("fsdp")

    hidden_far = send(hidden_in, lambda x, zl, c, y, zh: (x, zl, c, y, 1 - zh))

    parts = out_grad.reshape(tokens, 2, CORES, rows)
    even, odd = parts[:, :, 0], parts[:, :, 1]
    keep = jnp.where(core == 0, even, odd).reshape(tokens, 2 * rows)
    give = jnp.where(core == 0, odd, even).reshape(tokens, 2 * rows)
    grad_near = jnp.concatenate([keep, other_core(give)], axis=0)
    grads = [grad_near] + [
        send(grad_near, lambda x, zl, c, y, zh, d=d: (x, zl, c, (y - d) % NY, zh)) for d in (1, 2, 3)
    ]

    attn = attend_local(
        given_queries, given_keys, given_values, stored_keys, stored_values, cache_fill_length
    )
    row_count, step_count = attn.shape[0], attn.shape[1]
    every_attn = lax.all_gather(
        attn.reshape(row_count * step_count, width), "fsdp", axis=0, tiled=True
    )

    mine, theirs = chip_advantage(rewards, group_ids, position, core)
    scale = jnp.repeat(jnp.concatenate([mine, theirs]), tokens // rewards.shape[0])[:, None]

    def weighted(hidden):
        both = jnp.concatenate([hidden, other_core(hidden)], axis=0)
        return (both.astype(jnp.float32) * scale / seqs).astype(jnp.bfloat16)

    halves = []
    for hidden in (hidden_in, hidden_far):
        factor = weighted(hidden)
        tiles = jnp.stack(
            [
                lax.dot_general(
                    g, factor, (((0,), (0,)), ((), ())), preferred_element_type=jnp.float32
                ).astype(jnp.bfloat16)
                for g in grads
            ]
        )
        total = None
        for s in range(NX):
            tile = lax.dynamic_index_in_dim(tiles, (x + s - y) % NX, 0, keepdims=False)
            if s:
                tile = send(tile, lambda x, zl, c, y, zh, s=s: ((x + s) % NX, zl, c, y, zh))
            tile = tile.astype(jnp.float32)
            total = tile if total is None else total + tile
        halves.append(total.astype(jnp.bfloat16).reshape(2, rows, width))

    near, far = halves
    blocks = jnp.concatenate(
        [jnp.where(zh == 0, near, far), jnp.where(zh == 0, far, near)], axis=0
    )
    gradient = None
    for s in range(4):
        block = lax.dynamic_index_in_dim(blocks, zl ^ s, 0, keepdims=False)
        block = send(
            block,
            lambda x, zl, c, y, zh, s=s: (x, 2 * zh + ((zl ^ s) & 1), c, y, (zl ^ s) >> 1),
        ).astype(jnp.float32)
        gradient = block if gradient is None else gradient + block

    new_m = beta_one * adam_m + (1.0 - beta_one) * gradient
    new_v = beta_two * adam_v + (1.0 - beta_two) * gradient * gradient
    correct_one = 1.0 - beta_one**OPT_STEP
    correct_two = 1.0 - beta_two**OPT_STEP
    update = new_m / correct_one / (jnp.sqrt(new_v / correct_two) + adam_eps)
    new_weight = (
        weight.astype(jnp.float32) * (1.0 - learn_rate * decay_rate) - learn_rate * update
    ).astype(jnp.bfloat16)

    partial_out = lax.dot_general(
        every_attn, new_weight, (((1,), (1,)), ((), ())), preferred_element_type=jnp.float32
    ).astype(jnp.bfloat16)
    partial_out = partial_out.reshape(NY, -1, rows)
    summed = None
    for s in range(NY):
        block = lax.dynamic_index_in_dim(partial_out, y ^ s, 0, keepdims=False)
        block = send(block, lambda x, zl, c, y, zh, s=s: (y ^ s, zl, c, x, zh)).astype(jnp.float32)
        summed = block if summed is None else summed + block
    summed = summed.reshape(ZH, -1, rows)
    keep = lax.dynamic_index_in_dim(summed, zh, 0, keepdims=False)
    give = lax.dynamic_index_in_dim(summed, 1 - zh, 0, keepdims=False)
    summed = keep + send(give, lambda x, zl, c, y, zh: (x, zl, c, y, 1 - zh))
    summed = summed.reshape(4, -1, rows)
    place = (zl % 2) * CORES + core
    got = []
    for s in range(4):
        block = lax.dynamic_index_in_dim(summed, place ^ s, 0, keepdims=False)

        def dest(x, zl, c, y, zh, s=s):
            at = ((zl % 2) * CORES + c) ^ s
            return (x, 2 * zh + at // CORES, at % CORES, y, zl // 2)

        got.append(send(block, dest))
    got = jnp.stack(got)
    columns = [lax.dynamic_index_in_dim(got, place ^ j, 0, keepdims=False) for j in range(4)]
    layer_out = jnp.concatenate(columns, axis=1).reshape(row_count, step_count, width)
    return (new_weight, new_m, new_v, layer_out)


def solution(mesh):
    in_specs = (
        P("fsdp", "tp"),
        P("fsdp", "tp"),
        P("fsdp"),
        P(),
        P("fsdp", "tp"),
        P("fsdp", "tp"),
        P("fsdp", "tp"),
        P("fsdp", None, "tp"),
        P("fsdp", None, "tp"),
        P("fsdp", None, "tp"),
        P("fsdp", "tp", None, None),
        P("fsdp", "tp", None, None),
        P("fsdp"),
    )
    out_specs = (P("fsdp", "tp"), P("fsdp", "tp"), P("fsdp", "tp"), P("fsdp", None, "tp"))
    return jax.shard_map(
        per_device, mesh=mesh, in_specs=in_specs, out_specs=out_specs, check_vma=False
    )
```

```python
import math

import jax
import jax.numpy as jnp
from jax import lax
from jax.sharding import PartitionSpec as P

GSIZE = 8
OPT_STEP = 10

beta_one = 0.9
beta_two = 0.95
adam_eps = 1e-08
learn_rate = 0.002
decay_rate = 0.1
std_floor = 0.75

NX, ZL, CORES, NY, ZH = 4, 4, 2, 4, 2


def send(value, dest):
    pairs = []
    for x in range(NX):
        for zl in range(ZL):
            for c in range(CORES):
                for y in range(NY):
                    for zh in range(ZH):
                        to = dest(x, zl, c, y, zh)
                        pairs.append((flat(x, zl, c, y, zh), flat(*to)))
    return lax.ppermute(value, ("fsdp", "tp"), pairs)


def flat(x, zl, c, y, zh):
    return ((x * ZL + zl) * CORES + c) * (NY * ZH) + y * ZH + zh


def other_core(value):
    return send(value, lambda x, zl, c, y, zh: (x, zl, 1 - c, y, zh))


def attend_local(query_in, key_new, value_new, key_cache, value_cache, lengths):
    row_count = query_in.shape[0]
    step_count = query_in.shape[1]
    kv_heads = key_cache.shape[1]
    cache_size = key_cache.shape[2]
    head_dim = key_cache.shape[3]
    group_size = query_in.shape[2] // (kv_heads * head_dim)
    scaling = 1.0 / math.sqrt(head_dim)
    query_heads = query_in.reshape(row_count, step_count, kv_heads, group_size, head_dim)
    fresh_keys = key_new.reshape(row_count, step_count, kv_heads, head_dim)
    fresh_values = value_new.reshape(row_count, step_count, kv_heads, head_dim)
    cache_score = (
        jnp.einsum("rsKgd,rKcd->rKgsc", query_heads, key_cache, preferred_element_type=jnp.float32)
        * scaling
    )
    fresh_score = (
        jnp.einsum("rsKgd,rtKd->rKgst", query_heads, fresh_keys, preferred_element_type=jnp.float32)
        * scaling
    )
    cache_mask = jnp.arange(cache_size, dtype=jnp.int32)[None, :] < lengths[:, None]
    step_index = jnp.arange(step_count, dtype=jnp.int32)
    fresh_mask = step_index[None, :] <= step_index[:, None]
    cache_score = jnp.where(cache_mask[:, None, None, None, :], cache_score, -jnp.inf)
    fresh_score = jnp.where(fresh_mask, fresh_score, -jnp.inf)
    peak_score = jnp.maximum(
        jnp.max(cache_score, axis=-1, keepdims=True), jnp.max(fresh_score, axis=-1, keepdims=True)
    )
    cache_exp = jnp.exp(cache_score - peak_score)
    fresh_exp = jnp.exp(fresh_score - peak_score)
    total_exp = jnp.sum(cache_exp, axis=-1, keepdims=True) + jnp.sum(
        fresh_exp, axis=-1, keepdims=True
    )
    cache_prob = (cache_exp / total_exp).astype(jnp.bfloat16)
    fresh_prob = (fresh_exp / total_exp).astype(jnp.bfloat16)
    mixed = jnp.einsum(
        "rKgsc,rKcd->rsKgd", cache_prob, value_cache, preferred_element_type=jnp.float32
    )
    mixed = mixed + jnp.einsum(
        "rKgst,rtKd->rsKgd", fresh_prob, fresh_values, preferred_element_type=jnp.float32
    )
    return mixed.reshape(row_count, step_count, kv_heads * group_size * head_dim).astype(
        jnp.bfloat16
    )


def every_device(value):
    value = value + other_core(value)
    value = value + sum(
        send(value, lambda x, zl, c, y, zh, s=s: ((x + s) % NX, zl, c, y, zh)) for s in (1, 2, 3)
    )
    return value + sum(
        send(value, lambda x, zl, c, y, zh, s=s: (x, (zl + s) % ZL, c, y, zh)) for s in (1, 2, 3)
    )


def chip_advantage(rewards, group_ids, position, core):
    seq_dev = rewards.shape[0]
    seqs = seq_dev * lax.axis_size("fsdp")
    group_count = seqs // GSIZE
    spot = jnp.zeros((1, seqs), jnp.float32)
    spot = lax.dynamic_update_slice(spot, rewards[None, :], (0, position * seq_dev))
    every_reward = every_device(spot)[0]
    labels = jnp.arange(group_count, dtype=jnp.int32)
    member = (group_ids[:, None] == labels[None, :]).astype(jnp.float32)
    group_mean = jnp.sum(member * every_reward[:, None], axis=0) / GSIZE
    spread = every_reward - jnp.sum(member * group_mean[None, :], axis=1)
    group_var = jnp.sum(member * (spread * spread)[:, None], axis=0) / (GSIZE - 1)
    own_std = jnp.sqrt(jnp.sum(member * group_var[None, :], axis=1))
    advantage = spread / jnp.maximum(own_std, std_floor)
    mine = lax.dynamic_slice_in_dim(advantage, position * seq_dev, seq_dev)
    theirs = lax.dynamic_slice_in_dim(advantage, (position + 1 - 2 * core) * seq_dev, seq_dev)
    return mine, theirs


def per_device(
    hidden_in,
    out_grad,
    rewards,
    group_ids,
    weight,
    adam_m,
    adam_v,
    given_queries,
    given_keys,
    given_values,
    stored_keys,
    stored_values,
    cache_fill_length,
):
    position = lax.axis_index("fsdp")
    tp_at = lax.axis_index("tp")
    x, zl, core = position // (ZL * CORES), (position // CORES) % ZL, position % CORES
    y, zh = tp_at // ZH, tp_at % ZH
    tokens, width = hidden_in.shape
    rows = weight.shape[0]
    seqs = rewards.shape[0] * lax.axis_size("fsdp")

    hidden_far = send(hidden_in, lambda x, zl, c, y, zh: (x, zl, c, y, 1 - zh))

    turned = out_grad.T.reshape(2, CORES, rows, tokens)
    keep = lax.dynamic_index_in_dim(turned, core, 1, keepdims=False)
    give = lax.dynamic_index_in_dim(turned, 1 - core, 1, keepdims=False)
    near = jnp.concatenate([keep, other_core(give)], axis=2)
    same_zh = [[y * ZH + zh for y in range(NY)] for zh in range(ZH)]
    grads = [
        lax.all_gather(near[e], "tp", axis=0, axis_index_groups=same_zh).reshape(
            NY * rows, CORES * tokens
        )
        for e in range(2)
    ]

    attn = attend_local(
        given_queries, given_keys, given_values, stored_keys, stored_values, cache_fill_length
    )
    row_count, step_count = attn.shape[0], attn.shape[1]
    attn = attn.reshape(row_count * step_count, width)
    attn, grads = lax.optimization_barrier((attn, grads))
    every_attn = lax.all_gather(attn, "fsdp", axis=0, tiled=True)

    mine, theirs = chip_advantage(rewards, group_ids, position, core)
    scale = jnp.repeat(jnp.concatenate([mine, theirs]), tokens // rewards.shape[0])[:, None]

    def weighted(hidden):
        both = jnp.concatenate([hidden, other_core(hidden)], axis=0)
        both = (both.astype(jnp.float32) * scale / seqs).astype(jnp.bfloat16)
        return lax.optimization_barrier(both)

    def product(grad, factor):
        out = lax.dot_general(
            grad, factor, (((1,), (0,)), ((), ())), preferred_element_type=jnp.float32
        )
        return out.astype(jnp.bfloat16).reshape(NX, rows, -1)

    def over_x(tiles):
        total = None
        for s in range(NX):
            tile = lax.dynamic_index_in_dim(tiles, (x + s) % NX, 0, keepdims=False)
            if s:
                tile = send(tile, lambda x, zl, c, y, zh, s=s: ((x + s) % NX, zl, c, y, zh))
            tile = tile.astype(jnp.float32)
            total = tile if total is None else total + tile
        return total.astype(jnp.bfloat16)

    own_factor = weighted(hidden_in)
    own_sum = [over_x(product(g, own_factor)) for g in grads]
    far_factor = weighted(hidden_far)

    pieces = []
    for at, size in ((0, 384), (384, 256)):
        factor = far_factor[:, at : at + size]
        far = over_x(jnp.concatenate([product(g, factor) for g in grads], axis=1))
        far = far.reshape(2, rows, size)
        own = jnp.stack([part[:, at : at + size] for part in own_sum])
        blocks = jnp.concatenate(
            [jnp.where(zh == 0, own, far), jnp.where(zh == 0, far, own)], axis=0
        )
        piece = None
        for s in range(4):
            block = lax.dynamic_index_in_dim(blocks, zl ^ s, 0, keepdims=False)
            block = send(
                block,
                lambda x, zl, c, y, zh, s=s: (x, 2 * zh + ((zl ^ s) & 1), c, y, (zl ^ s) >> 1),
            ).astype(jnp.float32)
            piece = block if piece is None else piece + block
        pieces.append(piece)
    gradient = jnp.concatenate(pieces, axis=1)

    new_m = beta_one * adam_m + (1.0 - beta_one) * gradient
    new_v = beta_two * adam_v + (1.0 - beta_two) * gradient * gradient
    correct_one = 1.0 - beta_one**OPT_STEP
    correct_two = 1.0 - beta_two**OPT_STEP
    update = new_m / correct_one / (jnp.sqrt(new_v / correct_two) + adam_eps)
    new_weight = (
        weight.astype(jnp.float32) * (1.0 - learn_rate * decay_rate) - learn_rate * update
    ).astype(jnp.bfloat16)

    partial_out = lax.dot_general(
        new_weight, every_attn, (((1,), (1,)), ((), ())), preferred_element_type=jnp.float32
    ).astype(jnp.bfloat16)
    span = partial_out.shape[1] // NY
    summed = None
    for s in range(NY):
        block = lax.dynamic_slice_in_dim(partial_out, (y ^ s) * span, span, 1)
        block = send(block, lambda x, zl, c, y, zh, s=s: (y ^ s, zl, c, x, zh)).astype(jnp.float32)
        summed = block if summed is None else summed + block
    summed = summed.astype(jnp.bfloat16).reshape(2, rows // 2, ZL * CORES, -1)
    summed = summed.transpose(2, 1, 0, 3).reshape(ZL * CORES, rows // 2, -1)
    place = (zl % 2) * CORES + core
    got = []
    for s in range(4):
        pair = []
        for flip in range(2):
            block = lax.dynamic_index_in_dim(
                summed, (zh ^ flip) * 4 + (place ^ s), 0, keepdims=False
            )

            def dest(x, zl, c, y, zh, s=s, flip=flip):
                at = ((zl % 2) * CORES + c) ^ s
                return (x, 2 * (zh ^ flip) + at // CORES, at % CORES, y, zl // 2)

            pair.append(send(block, dest).astype(jnp.float32))
        got.append(pair[0] + pair[1])
    got = jnp.stack(got)
    got = jnp.stack(
        [lax.dynamic_index_in_dim(got, place ^ j, 0, keepdims=False) for j in range(4)]
    )
    got = got.reshape(4, rows // 2, 2, row_count * step_count)
    layer_out = got.transpose(3, 0, 2, 1).reshape(row_count, step_count, width)
    return (new_weight, new_m, new_v, layer_out)


def solution(mesh):
    in_specs = (
        P("fsdp", "tp"),
        P("fsdp", "tp"),
        P("fsdp"),
        P(),
        P("fsdp", "tp"),
        P("fsdp", "tp"),
        P("fsdp", "tp"),
        P("fsdp", None, "tp"),
        P("fsdp", None, "tp"),
        P("fsdp", None, "tp"),
        P("fsdp", "tp", None, None),
        P("fsdp", "tp", None, None),
        P("fsdp"),
    )
    out_specs = (P("fsdp", "tp"), P("fsdp", "tp"), P("fsdp", "tp"), P("fsdp", None, "tp"))
    return jax.shard_map(
        per_device, mesh=mesh, in_specs=in_specs, out_specs=out_specs, check_vma=False
    )
```

```python
import math

import jax
import jax.numpy as jnp
from jax import lax
from jax.sharding import PartitionSpec as P

GSIZE = 8
OPT_STEP = 10

beta_one = 0.9
beta_two = 0.95
adam_eps = 1e-08
learn_rate = 0.002
decay_rate = 0.1
std_floor = 0.75

NX, ZL, CORES, NY, ZH = 4, 4, 2, 4, 2
SPANS = ((0, 384), (384, 256))


def send(value, dest):
    pairs = []
    for x in range(NX):
        for zl in range(ZL):
            for c in range(CORES):
                for y in range(NY):
                    for zh in range(ZH):
                        to = dest(x, zl, c, y, zh)
                        pairs.append((flat(x, zl, c, y, zh), flat(*to)))
    return lax.ppermute(value, ("fsdp", "tp"), pairs)


def flat(x, zl, c, y, zh):
    return ((x * ZL + zl) * CORES + c) * (NY * ZH) + y * ZH + zh


def other_core(value):
    return send(value, lambda x, zl, c, y, zh: (x, zl, 1 - c, y, zh))


def attend_local(query_in, key_new, value_new, key_cache, value_cache, lengths):
    row_count = query_in.shape[0]
    step_count = query_in.shape[1]
    kv_heads = key_cache.shape[1]
    cache_size = key_cache.shape[2]
    head_dim = key_cache.shape[3]
    group_size = query_in.shape[2] // (kv_heads * head_dim)
    scaling = 1.0 / math.sqrt(head_dim)
    query_heads = query_in.reshape(row_count, step_count, kv_heads, group_size, head_dim)
    fresh_keys = key_new.reshape(row_count, step_count, kv_heads, head_dim)
    fresh_values = value_new.reshape(row_count, step_count, kv_heads, head_dim)
    cache_score = (
        jnp.einsum("rsKgd,rKcd->rKgsc", query_heads, key_cache, preferred_element_type=jnp.float32)
        * scaling
    )
    fresh_score = (
        jnp.einsum("rsKgd,rtKd->rKgst", query_heads, fresh_keys, preferred_element_type=jnp.float32)
        * scaling
    )
    cache_mask = jnp.arange(cache_size, dtype=jnp.int32)[None, :] < lengths[:, None]
    step_index = jnp.arange(step_count, dtype=jnp.int32)
    fresh_mask = step_index[None, :] <= step_index[:, None]
    cache_score = jnp.where(cache_mask[:, None, None, None, :], cache_score, -jnp.inf)
    fresh_score = jnp.where(fresh_mask, fresh_score, -jnp.inf)
    peak_score = jnp.maximum(
        jnp.max(cache_score, axis=-1, keepdims=True), jnp.max(fresh_score, axis=-1, keepdims=True)
    )
    cache_exp = jnp.exp(cache_score - peak_score)
    fresh_exp = jnp.exp(fresh_score - peak_score)
    total_exp = jnp.sum(cache_exp, axis=-1, keepdims=True) + jnp.sum(
        fresh_exp, axis=-1, keepdims=True
    )
    cache_prob = (cache_exp / total_exp).astype(jnp.bfloat16)
    fresh_prob = (fresh_exp / total_exp).astype(jnp.bfloat16)
    mixed = jnp.einsum(
        "rKgsc,rKcd->rsKgd", cache_prob, value_cache, preferred_element_type=jnp.float32
    )
    mixed = mixed + jnp.einsum(
        "rKgst,rtKd->rsKgd", fresh_prob, fresh_values, preferred_element_type=jnp.float32
    )
    return mixed.reshape(row_count, step_count, kv_heads * group_size * head_dim).astype(
        jnp.bfloat16
    )


def chip_sequences(rewards, every_reward, group_ids, position, core):
    seq_dev = rewards.shape[0]
    seqs = seq_dev * lax.axis_size("fsdp")
    group_count = seqs // GSIZE
    labels = jnp.arange(group_count, dtype=jnp.int32)
    member = (group_ids[:, None] == labels[None, :]).astype(jnp.float32)
    group_mean = jnp.sum(member * every_reward[:, None], axis=0) / GSIZE
    spread = every_reward - jnp.sum(member * group_mean[None, :], axis=1)
    group_var = jnp.sum(member * (spread * spread)[:, None], axis=0) / (GSIZE - 1)
    own_std = jnp.sqrt(jnp.sum(member * group_var[None, :], axis=1))
    advantage = spread / jnp.maximum(own_std, std_floor)
    mine = lax.dynamic_slice_in_dim(advantage, position * seq_dev, seq_dev)
    theirs = lax.dynamic_slice_in_dim(advantage, (position + 1 - 2 * core) * seq_dev, seq_dev)
    return mine, theirs


def per_device(
    hidden_in,
    out_grad,
    rewards,
    group_ids,
    weight,
    adam_m,
    adam_v,
    given_queries,
    given_keys,
    given_values,
    stored_keys,
    stored_values,
    cache_fill_length,
):
    position = lax.axis_index("fsdp")
    tp_at = lax.axis_index("tp")
    x, zl, core = position // (ZL * CORES), (position // CORES) % ZL, position % CORES
    y, zh = tp_at // ZH, tp_at % ZH
    tokens, width = hidden_in.shape
    rows = weight.shape[0]
    seqs = rewards.shape[0] * lax.axis_size("fsdp")

    turned = out_grad.T.reshape(2, CORES, rows, tokens)
    keep = lax.dynamic_index_in_dim(turned, core, 1, keepdims=False)
    give = lax.dynamic_index_in_dim(turned, 1 - core, 1, keepdims=False)
    near = jnp.concatenate([keep, other_core(give)], axis=2)

    spot = jnp.zeros((1, seqs), jnp.float32)
    spot = lax.dynamic_update_slice(spot, rewards[None, :], (0, position * rewards.shape[0]))
    spot = spot + sum(
        send(spot, lambda x, zl, c, y, zh, s=s: (x ^ s, zl, c, y, zh)) for s in (1, 2, 3)
    )
    spot = spot + other_core(spot)
    high = lax.reduce_precision(spot, 8, 7)
    middle = lax.reduce_precision(spot - high, 8, 7)
    spot = jnp.concatenate([high, middle, spot - high - middle]).astype(jnp.bfloat16)

    attn = attend_local(
        given_queries, given_keys, given_values, stored_keys, stored_values, cache_fill_length
    )
    row_count, step_count = attn.shape[0], attn.shape[1]
    attn = attn.reshape(row_count * step_count, width)
    load = jnp.concatenate([attn, jnp.pad(spot, ((0, 13), (0, width - seqs)))])
    load, near = lax.optimization_barrier((load, near))
    loads = jnp.stack(
        [load] + [send(load, lambda x, zl, c, y, zh, s=s: (x, zl ^ s, c, y, zh)) for s in (1, 2, 3)]
    )

    hidden_in, loads = lax.optimization_barrier((hidden_in, loads))
    far = send(hidden_in, lambda x, zl, c, y, zh: (x, zl, c, y, 1 - zh))

    def down(value):
        return send(value, lambda x, zl, c, y, zh: (x, zl, c, (y - 1) % NY, zh))

    def up(value):
        return send(value, lambda x, zl, c, y, zh: (x, zl, c, (y + 1) % NY, zh))

    after, before = down(near), up(near)
    across = [down(after[0]), up(before[1])]

    spot = jnp.sum(loads[:, attn.shape[0] : attn.shape[0] + 3, :seqs].astype(jnp.float32), axis=1)
    spot = jnp.sum(spot, axis=0, keepdims=True)
    mine, theirs = chip_sequences(rewards, spot[0], group_ids, position, core)
    scale = jnp.repeat(jnp.concatenate([mine, theirs]), tokens // rewards.shape[0])[None, :] / seqs

    def scaled(block):
        block = (block.astype(jnp.float32) * scale).astype(jnp.bfloat16)
        return lax.optimization_barrier(block.reshape(2 * rows, CORES * tokens))

    grads = [scaled(near), scaled(after), scaled(jnp.stack(across)), scaled(before)]

    near_attn = jnp.concatenate(
        [
            lax.dynamic_index_in_dim(loads, zl ^ j, 0, keepdims=False)[: attn.shape[0]]
            for j in range(ZL)
        ]
    )
    by_xc = [
        [flat(x, zl, c, 0, 0) // (NY * ZH) for x in range(NX) for c in range(CORES)]
        for zl in range(ZL)
    ]
    every_attn = lax.all_gather(near_attn, "fsdp", axis=0, tiled=True, axis_index_groups=by_xc)

    def both_cores(hidden):
        return jnp.concatenate([hidden, other_core(hidden)], axis=0)

    def product(factor):
        return jnp.stack(
            [
                lax.dot_general(
                    grad, factor, (((1,), (0,)), ((), ())), preferred_element_type=jnp.float32
                ).astype(jnp.bfloat16)
                for grad in grads
            ]
        )

    def to_x(tiles):
        got = []
        for s in range(NX):
            tile = lax.dynamic_index_in_dim(tiles, (x + s - y) % NX, 0, keepdims=False)
            if s:
                tile = send(tile, lambda x, zl, c, y, zh, s=s: ((x + s) % NX, zl, c, y, zh))
            got.append(tile)
        return got

    def added(tiles):
        return sum(tile.astype(jnp.float32) for tile in tiles).reshape(2, rows, -1)

    tiles = product(lax.optimization_barrier(both_cores(hidden_in)))
    own = to_x(tiles)
    far, own = lax.optimization_barrier((far, own))
    own_sum = added(own)
    far = both_cores(far)
    far_sums = []
    for at, size in SPANS:
        tiles = product(far[:, at : at + size])
        far_sums.append(added(to_x(tiles)))
        far, _ = lax.optimization_barrier((far, tiles))

    pieces = []
    for (at, size), far in zip(SPANS, far_sums, strict=True):
        own = own_sum[:, :, at : at + size]
        blocks = jnp.stack([jnp.where(zh == 0, own, far), jnp.where(zh == 0, far, own)])
        low = zl % 2
        keep = lax.dynamic_index_in_dim(blocks, low, 1, keepdims=False)
        give = lax.dynamic_index_in_dim(blocks, 1 - low, 1, keepdims=False)
        give = give.astype(jnp.bfloat16)
        keep = keep + send(give, lambda x, zl, c, y, zh: (x, zl ^ 1, c, y, zh)).astype(jnp.float32)
        piece = None
        for s in range(2):
            block = lax.dynamic_index_in_dim(keep, (zl // 2) ^ s, 0, keepdims=False)
            block = send(
                block.astype(jnp.bfloat16),
                lambda x, zl, c, y, zh, s=s: (x, 2 * zh + zl % 2, c, y, (zl // 2) ^ s),
            ).astype(jnp.float32)
            piece = block if piece is None else piece + block
        pieces.append(piece)
    gradient = jnp.concatenate(pieces, axis=1)

    new_m = beta_one * adam_m + (1.0 - beta_one) * gradient
    new_v = beta_two * adam_v + (1.0 - beta_two) * gradient * gradient
    correct_one = 1.0 - beta_one**OPT_STEP
    correct_two = 1.0 - beta_two**OPT_STEP
    update = new_m / correct_one / (jnp.sqrt(new_v / correct_two) + adam_eps)
    new_weight = (
        weight.astype(jnp.float32) * (1.0 - learn_rate * decay_rate) - learn_rate * update
    ).astype(jnp.bfloat16)

    partial_out = lax.dot_general(
        new_weight, every_attn, (((1,), (1,)), ((), ())), preferred_element_type=jnp.float32
    ).astype(jnp.bfloat16)
    span = partial_out.shape[1] // NY
    summed = None
    for s in range(NY):
        block = lax.dynamic_slice_in_dim(partial_out, (y ^ s) * span, span, 1)
        block = send(block, lambda x, zl, c, y, zh, s=s: (y ^ s, zl, c, x, zh)).astype(jnp.float32)
        summed = block if summed is None else summed + block
    summed = summed.astype(jnp.bfloat16).reshape(2, rows // 2, CORES, ZL, -1)
    summed = summed.transpose(3, 2, 1, 0, 4).reshape(ZL * CORES, 1, rows // 2, -1)
    low = (zl < ZL // 2)
    none = jnp.zeros_like(summed)
    summed = jnp.concatenate(
        [jnp.where(low, summed, none), jnp.where(low, none, summed)], axis=1
    ).reshape(ZL * CORES * ZH, rows // 2, -1)
    in_column = [
        [flat(x, zl, c, y, zh) for zl in range(ZL) for c in range(CORES) for zh in range(ZH)]
        for x in range(NX)
        for y in range(NY)
    ]
    got = lax.all_to_all(
        summed, ("fsdp", "tp"), 0, 0, axis_index_groups=in_column, tiled=True
    )
    got = got.reshape(2, 4, ZH, rows // 2, 2, row_count * step_count)
    got = lax.dynamic_index_in_dim(got, zh, 0, keepdims=False).astype(jnp.float32)
    layer_out = (got[:, 0] + got[:, 1]).transpose(3, 0, 2, 1)
    layer_out = layer_out.reshape(row_count, step_count, width)
    return (new_weight, new_m, new_v, layer_out)


def solution(mesh):
    in_specs = (
        P("fsdp", "tp"),
        P("fsdp", "tp"),
        P("fsdp"),
        P(),
        P("fsdp", "tp"),
        P("fsdp", "tp"),
        P("fsdp", "tp"),
        P("fsdp", None, "tp"),
        P("fsdp", None, "tp"),
        P("fsdp", None, "tp"),
        P("fsdp", "tp", None, None),
        P("fsdp", "tp", None, None),
        P("fsdp"),
    )
    out_specs = (P("fsdp", "tp"), P("fsdp", "tp"), P("fsdp", "tp"), P("fsdp", None, "tp"))
    return jax.shard_map(
        per_device, mesh=mesh, in_specs=in_specs, out_specs=out_specs, check_vma=False
    )
```

```python
import math

import jax
import jax.numpy as jnp
from jax import lax
from jax.sharding import PartitionSpec as P

GSIZE = 8
OPT_STEP = 10

beta_one = 0.9
beta_two = 0.95
adam_eps = 1e-08
learn_rate = 0.002
decay_rate = 0.1
std_floor = 0.75

NX, ZL, CORES, NY, ZH = 4, 4, 2, 4, 2
SPANS = ((0, 384), (384, 256))


def send(value, dest):
    pairs = []
    for x in range(NX):
        for zl in range(ZL):
            for c in range(CORES):
                for y in range(NY):
                    for zh in range(ZH):
                        to = dest(x, zl, c, y, zh)
                        pairs.append((flat(x, zl, c, y, zh), flat(*to)))
    return lax.ppermute(value, ("fsdp", "tp"), pairs)


def flat(x, zl, c, y, zh):
    return ((x * ZL + zl) * CORES + c) * (NY * ZH) + y * ZH + zh


def other_core(value):
    return send(value, lambda x, zl, c, y, zh: (x, zl, 1 - c, y, zh))


def attend_local(query_in, key_new, value_new, key_cache, value_cache, lengths):
    row_count = query_in.shape[0]
    step_count = query_in.shape[1]
    kv_heads = key_cache.shape[1]
    cache_size = key_cache.shape[2]
    head_dim = key_cache.shape[3]
    group_size = query_in.shape[2] // (kv_heads * head_dim)
    scaling = 1.0 / math.sqrt(head_dim)
    query_heads = query_in.reshape(row_count, step_count, kv_heads, group_size, head_dim)
    fresh_keys = key_new.reshape(row_count, step_count, kv_heads, head_dim)
    fresh_values = value_new.reshape(row_count, step_count, kv_heads, head_dim)
    cache_score = (
        jnp.einsum("rsKgd,rKcd->rKgsc", query_heads, key_cache, preferred_element_type=jnp.float32)
        * scaling
    )
    fresh_score = (
        jnp.einsum("rsKgd,rtKd->rKgst", query_heads, fresh_keys, preferred_element_type=jnp.float32)
        * scaling
    )
    cache_mask = jnp.arange(cache_size, dtype=jnp.int32)[None, :] < lengths[:, None]
    step_index = jnp.arange(step_count, dtype=jnp.int32)
    fresh_mask = step_index[None, :] <= step_index[:, None]
    cache_score = jnp.where(cache_mask[:, None, None, None, :], cache_score, -jnp.inf)
    fresh_score = jnp.where(fresh_mask, fresh_score, -jnp.inf)
    peak_score = jnp.maximum(
        jnp.max(cache_score, axis=-1, keepdims=True), jnp.max(fresh_score, axis=-1, keepdims=True)
    )
    cache_exp = jnp.exp(cache_score - peak_score)
    fresh_exp = jnp.exp(fresh_score - peak_score)
    total_exp = jnp.sum(cache_exp, axis=-1, keepdims=True) + jnp.sum(
        fresh_exp, axis=-1, keepdims=True
    )
    cache_prob = (cache_exp / total_exp).astype(jnp.bfloat16)
    fresh_prob = (fresh_exp / total_exp).astype(jnp.bfloat16)
    mixed = jnp.einsum(
        "rKgsc,rKcd->rsKgd", cache_prob, value_cache, preferred_element_type=jnp.float32
    )
    mixed = mixed + jnp.einsum(
        "rKgst,rtKd->rsKgd", fresh_prob, fresh_values, preferred_element_type=jnp.float32
    )
    return mixed.reshape(row_count, step_count, kv_heads * group_size * head_dim).astype(
        jnp.bfloat16
    )


def chip_sequences(rewards, every_reward, group_ids, position, core):
    seq_dev = rewards.shape[0]
    seqs = seq_dev * lax.axis_size("fsdp")
    group_count = seqs // GSIZE
    labels = jnp.arange(group_count, dtype=jnp.int32)
    member = (group_ids[:, None] == labels[None, :]).astype(jnp.float32)
    group_mean = jnp.sum(member * every_reward[:, None], axis=0) / GSIZE
    spread = every_reward - jnp.sum(member * group_mean[None, :], axis=1)
    group_var = jnp.sum(member * (spread * spread)[:, None], axis=0) / (GSIZE - 1)
    own_std = jnp.sqrt(jnp.sum(member * group_var[None, :], axis=1))
    advantage = spread / jnp.maximum(own_std, std_floor)
    mine = lax.dynamic_slice_in_dim(advantage, position * seq_dev, seq_dev)
    theirs = lax.dynamic_slice_in_dim(advantage, (position + 1 - 2 * core) * seq_dev, seq_dev)
    return mine, theirs


def per_device(
    hidden_in,
    out_grad,
    rewards,
    group_ids,
    weight,
    adam_m,
    adam_v,
    given_queries,
    given_keys,
    given_values,
    stored_keys,
    stored_values,
    cache_fill_length,
):
    position = lax.axis_index("fsdp")
    tp_at = lax.axis_index("tp")
    x, zl, core = position // (ZL * CORES), (position // CORES) % ZL, position % CORES
    y, zh = tp_at // ZH, tp_at % ZH
    tokens, width = hidden_in.shape
    rows = weight.shape[0]
    seqs = rewards.shape[0] * lax.axis_size("fsdp")

    turned = out_grad.T.reshape(2, CORES, rows, tokens)
    keep = lax.dynamic_index_in_dim(turned, core, 1, keepdims=False)
    give = lax.dynamic_index_in_dim(turned, 1 - core, 1, keepdims=False)
    near = jnp.concatenate([keep, other_core(give)], axis=2).reshape(2 * rows, CORES * tokens)
    same_zh = [[y * ZH + zh for y in range(NY)] for zh in range(ZH)]
    every_grad = lax.all_gather(near, "tp", axis=0, tiled=True, axis_index_groups=same_zh)

    far_soon = send(hidden_in[:, : SPANS[0][1]], lambda x, zl, c, y, zh: (x, zl, c, y, 1 - zh))

    spot = jnp.zeros((1, seqs), jnp.float32)
    spot = lax.dynamic_update_slice(spot, rewards[None, :], (0, position * rewards.shape[0]))
    spot = spot + sum(
        send(spot, lambda x, zl, c, y, zh, s=s: (x ^ s, zl, c, y, zh)) for s in (1, 2, 3)
    )
    spot = spot + other_core(spot)
    high = lax.reduce_precision(spot, 8, 7)
    middle = lax.reduce_precision(spot - high, 8, 7)
    spot = jnp.concatenate([high, middle, spot - high - middle]).astype(jnp.bfloat16)

    attn = attend_local(
        given_queries, given_keys, given_values, stored_keys, stored_values, cache_fill_length
    )
    row_count, step_count = attn.shape[0], attn.shape[1]
    attn = attn.reshape(row_count * step_count, width)
    load = jnp.concatenate([attn, jnp.pad(spot, ((0, 13), (0, width - seqs)))])
    load, _ = lax.optimization_barrier((load, near))
    loads = load[None]
    for bit in (1, 2):
        got = send(loads, lambda x, zl, c, y, zh, bit=bit: (x, zl ^ bit, c, y, zh))
        upper = (zl & bit) != 0
        loads = jnp.concatenate(
            [jnp.where(upper, got, loads), jnp.where(upper, loads, got)], axis=0
        )

    late, loads = lax.optimization_barrier((hidden_in[:, SPANS[0][1] :], loads))
    far_late = send(late, lambda x, zl, c, y, zh: (x, zl, c, y, 1 - zh))

    spot = jnp.sum(loads[:, attn.shape[0] : attn.shape[0] + 3, :seqs].astype(jnp.float32), axis=1)
    spot = jnp.sum(spot, axis=0, keepdims=True)
    mine, theirs = chip_sequences(rewards, spot[0], group_ids, position, core)
    scale = jnp.repeat(jnp.concatenate([mine, theirs]), tokens // rewards.shape[0])[None, :] / seqs

    grads = (every_grad.astype(jnp.float32) * scale).astype(jnp.bfloat16)
    grads = lax.optimization_barrier(grads)

    near_attn = loads[:, : attn.shape[0]].reshape(1, -1, width)
    near_attn = [near_attn] + [
        send(near_attn, lambda x, zl, c, y, zh, s=s: (x ^ s, zl, c, y, zh)) for s in (1, 2, 3)
    ]

    def both_cores(hidden):
        return jnp.concatenate([hidden, other_core(hidden)], axis=0)

    def product(factor):
        out = lax.dot_general(
            grads, factor, (((1,), (0,)), ((), ())), preferred_element_type=jnp.float32
        )
        return out.astype(jnp.bfloat16).reshape(NY, 2 * rows, -1)

    def to_x(tiles):
        got = []
        for s in range(NX):
            tile = lax.dynamic_index_in_dim(tiles, (x + s) % NX, 0, keepdims=False)
            if s:
                tile = send(tile, lambda x, zl, c, y, zh, s=s: ((x + s) % NX, zl, c, y, zh))
            got.append(tile)
        return got

    def added(tiles):
        return sum(tile.astype(jnp.float32) for tile in tiles).reshape(2, rows, -1)

    tiles = product(lax.optimization_barrier(both_cores(hidden_in)))
    far_soon, near_attn, _ = lax.optimization_barrier((both_cores(far_soon), near_attn, tiles))
    own = to_x(tiles)
    soon = to_x(product(far_soon))
    far_late, own = lax.optimization_barrier((far_late, own))
    tiles = product(both_cores(far_late))
    far_sums = [added(soon), added(to_x(tiles))]
    own_sum = added(own)

    near_attn = jnp.concatenate(near_attn)
    got = other_core(near_attn)
    every_attn = jnp.stack(
        [jnp.where(core == 0, near_attn, got), jnp.where(core == 0, got, near_attn)], axis=1
    )
    every_attn = lax.optimization_barrier(every_attn.reshape(-1, width))

    pieces = []
    for (at, size), far in zip(SPANS, far_sums, strict=True):
        own = own_sum[:, :, at : at + size]
        blocks = jnp.stack([jnp.where(zh == 0, own, far), jnp.where(zh == 0, far, own)])
        low = zl % 2
        keep = lax.dynamic_index_in_dim(blocks, low, 1, keepdims=False)
        give = lax.dynamic_index_in_dim(blocks, 1 - low, 1, keepdims=False)
        give = give.astype(jnp.bfloat16)
        keep = keep + send(give, lambda x, zl, c, y, zh: (x, zl ^ 1, c, y, zh)).astype(jnp.float32)
        piece = None
        for s in range(2):
            block = lax.dynamic_index_in_dim(keep, (zl // 2) ^ s, 0, keepdims=False)
            block = send(
                block.astype(jnp.bfloat16),
                lambda x, zl, c, y, zh, s=s: (x, 2 * zh + zl % 2, c, y, (zl // 2) ^ s),
            ).astype(jnp.float32)
            piece = block if piece is None else piece + block
        pieces.append(piece)
    gradient = jnp.concatenate(pieces, axis=1)

    new_m = beta_one * adam_m + (1.0 - beta_one) * gradient
    new_v = beta_two * adam_v + (1.0 - beta_two) * gradient * gradient
    correct_one = 1.0 - beta_one**OPT_STEP
    correct_two = 1.0 - beta_two**OPT_STEP
    update = new_m / correct_one / (jnp.sqrt(new_v / correct_two) + adam_eps)
    new_weight = (
        weight.astype(jnp.float32) * (1.0 - learn_rate * decay_rate) - learn_rate * update
    ).astype(jnp.bfloat16)

    partial_out = lax.dot_general(
        new_weight, every_attn, (((1,), (1,)), ((), ())), preferred_element_type=jnp.float32
    ).astype(jnp.bfloat16)
    span = partial_out.shape[1] // NY
    summed = None
    for s in range(NY):
        block = lax.dynamic_slice_in_dim(partial_out, (x ^ y ^ s) * span, span, 1)
        block = send(block, lambda x, zl, c, y, zh, s=s: (y ^ s, zl, c, x, zh)).astype(jnp.float32)
        summed = block if summed is None else summed + block
    summed = summed.astype(jnp.bfloat16).reshape(2, rows // 2, CORES, ZL, -1)
    summed = summed.transpose(3, 2, 1, 0, 4).reshape(ZL * CORES, 1, rows // 2, -1)
    low = (zl < ZL // 2)
    none = jnp.zeros_like(summed)
    summed = jnp.concatenate(
        [jnp.where(low, summed, none), jnp.where(low, none, summed)], axis=1
    ).reshape(ZL * CORES * ZH, rows // 2, -1)
    in_column = [
        [flat(x, zl, c, y, zh) for zl in range(ZL) for c in range(CORES) for zh in range(ZH)]
        for x in range(NX)
        for y in range(NY)
    ]
    got = lax.all_to_all(
        summed, ("fsdp", "tp"), 0, 0, axis_index_groups=in_column, tiled=True
    )
    got = got.reshape(2, 4, ZH, rows // 2, 2, row_count * step_count)
    got = lax.dynamic_index_in_dim(got, zh, 0, keepdims=False).astype(jnp.float32)
    layer_out = (got[:, 0] + got[:, 1]).transpose(3, 0, 2, 1)
    layer_out = layer_out.reshape(row_count, step_count, width)
    return (new_weight, new_m, new_v, layer_out)


def solution(mesh):
    in_specs = (
        P("fsdp", "tp"),
        P("fsdp", "tp"),
        P("fsdp"),
        P(),
        P("fsdp", "tp"),
        P("fsdp", "tp"),
        P("fsdp", "tp"),
        P("fsdp", None, "tp"),
        P("fsdp", None, "tp"),
        P("fsdp", None, "tp"),
        P("fsdp", "tp", None, None),
        P("fsdp", "tp", None, None),
        P("fsdp"),
    )
    out_specs = (P("fsdp", "tp"), P("fsdp", "tp"), P("fsdp", "tp"), P("fsdp", None, "tp"))
    return jax.shard_map(
        per_device, mesh=mesh, in_specs=in_specs, out_specs=out_specs, check_vma=False
    )
```

```python
import math

import jax
import jax.numpy as jnp
from jax import lax
from jax.sharding import PartitionSpec as P

GSIZE = 8
OPT_STEP = 10

beta_one = 0.9
beta_two = 0.95
adam_eps = 1e-08
learn_rate = 0.002
decay_rate = 0.1
std_floor = 0.75

NX, ZL, CORES, NY, ZH = 4, 4, 2, 4, 2
SPANS = ((0, 384), (384, 256))


def send(value, dest):
    pairs = []
    for x in range(NX):
        for zl in range(ZL):
            for c in range(CORES):
                for y in range(NY):
                    for zh in range(ZH):
                        to = dest(x, zl, c, y, zh)
                        pairs.append((flat(x, zl, c, y, zh), flat(*to)))
    return lax.ppermute(value, ("fsdp", "tp"), pairs)


def flat(x, zl, c, y, zh):
    return ((x * ZL + zl) * CORES + c) * (NY * ZH) + y * ZH + zh


def other_core(value):
    return send(value, lambda x, zl, c, y, zh: (x, zl, 1 - c, y, zh))


def attend_local(query_in, key_new, value_new, key_cache, value_cache, lengths):
    row_count = query_in.shape[0]
    step_count = query_in.shape[1]
    kv_heads = key_cache.shape[1]
    cache_size = key_cache.shape[2]
    head_dim = key_cache.shape[3]
    group_size = query_in.shape[2] // (kv_heads * head_dim)
    scaling = 1.0 / math.sqrt(head_dim)
    query_heads = query_in.reshape(row_count, step_count, kv_heads, group_size, head_dim)
    fresh_keys = key_new.reshape(row_count, step_count, kv_heads, head_dim)
    fresh_values = value_new.reshape(row_count, step_count, kv_heads, head_dim)
    cache_score = (
        jnp.einsum("rsKgd,rKcd->rKgsc", query_heads, key_cache, preferred_element_type=jnp.float32)
        * scaling
    )
    fresh_score = (
        jnp.einsum("rsKgd,rtKd->rKgst", query_heads, fresh_keys, preferred_element_type=jnp.float32)
        * scaling
    )
    cache_mask = jnp.arange(cache_size, dtype=jnp.int32)[None, :] < lengths[:, None]
    step_index = jnp.arange(step_count, dtype=jnp.int32)
    fresh_mask = step_index[None, :] <= step_index[:, None]
    cache_score = jnp.where(cache_mask[:, None, None, None, :], cache_score, -jnp.inf)
    fresh_score = jnp.where(fresh_mask, fresh_score, -jnp.inf)
    peak_score = jnp.maximum(
        jnp.max(cache_score, axis=-1, keepdims=True), jnp.max(fresh_score, axis=-1, keepdims=True)
    )
    cache_exp = jnp.exp(cache_score - peak_score)
    fresh_exp = jnp.exp(fresh_score - peak_score)
    total_exp = jnp.sum(cache_exp, axis=-1, keepdims=True) + jnp.sum(
        fresh_exp, axis=-1, keepdims=True
    )
    cache_prob = (cache_exp / total_exp).astype(jnp.bfloat16)
    fresh_prob = (fresh_exp / total_exp).astype(jnp.bfloat16)
    mixed = jnp.einsum(
        "rKgsc,rKcd->rsKgd", cache_prob, value_cache, preferred_element_type=jnp.float32
    )
    mixed = mixed + jnp.einsum(
        "rKgst,rtKd->rsKgd", fresh_prob, fresh_values, preferred_element_type=jnp.float32
    )
    return mixed.reshape(row_count, step_count, kv_heads * group_size * head_dim).astype(
        jnp.bfloat16
    )


def chip_sequences(rewards, every_reward, group_ids, position, core):
    seq_dev = rewards.shape[0]
    seqs = seq_dev * lax.axis_size("fsdp")
    group_count = seqs // GSIZE
    labels = jnp.arange(group_count, dtype=jnp.int32)
    member = (group_ids[:, None] == labels[None, :]).astype(jnp.float32)
    group_mean = jnp.sum(member * every_reward[:, None], axis=0) / GSIZE
    spread = every_reward - jnp.sum(member * group_mean[None, :], axis=1)
    group_var = jnp.sum(member * (spread * spread)[:, None], axis=0) / (GSIZE - 1)
    own_std = jnp.sqrt(jnp.sum(member * group_var[None, :], axis=1))
    advantage = spread / jnp.maximum(own_std, std_floor)
    mine = lax.dynamic_slice_in_dim(advantage, position * seq_dev, seq_dev)
    theirs = lax.dynamic_slice_in_dim(advantage, (position + 1 - 2 * core) * seq_dev, seq_dev)
    return mine, theirs


def per_device(
    hidden_in,
    out_grad,
    rewards,
    group_ids,
    weight,
    adam_m,
    adam_v,
    given_queries,
    given_keys,
    given_values,
    stored_keys,
    stored_values,
    cache_fill_length,
):
    position = lax.axis_index("fsdp")
    tp_at = lax.axis_index("tp")
    x, zl, core = position // (ZL * CORES), (position // CORES) % ZL, position % CORES
    y, zh = tp_at // ZH, tp_at % ZH
    tokens, width = hidden_in.shape
    rows = weight.shape[0]
    seqs = rewards.shape[0] * lax.axis_size("fsdp")

    turned = out_grad.T.reshape(2, CORES, rows, tokens)
    keep = lax.dynamic_index_in_dim(turned, core, 1, keepdims=False)
    give = lax.dynamic_index_in_dim(turned, 1 - core, 1, keepdims=False)
    near = jnp.concatenate([keep, other_core(give)], axis=2).reshape(2 * rows, CORES * tokens)
    same_zh = [[y * ZH + zh for y in range(NY)] for zh in range(ZH)]
    every_grad = lax.all_gather(near, "tp", axis=0, tiled=True, axis_index_groups=same_zh)

    far_soon = send(hidden_in[:, : SPANS[0][1]], lambda x, zl, c, y, zh: (x, zl, c, y, 1 - zh))

    spot = jnp.zeros((1, seqs), jnp.float32)
    spot = lax.dynamic_update_slice(spot, rewards[None, :], (0, position * rewards.shape[0]))
    spot = spot + sum(
        send(spot, lambda x, zl, c, y, zh, s=s: (x, zl ^ s, c, y, zh)) for s in (1, 2, 3)
    )
    spot = spot + sum(
        send(spot, lambda x, zl, c, y, zh, s=s: (x ^ s, zl, c, y, zh)) for s in (1, 2, 3)
    )
    spot = spot + other_core(spot)
    mine, theirs = chip_sequences(rewards, spot[0], group_ids, position, core)
    scale = jnp.concatenate([mine, theirs])[:, None, None]

    attn = attend_local(
        given_queries, given_keys, given_values, stored_keys, stored_values, cache_fill_length
    )
    row_count, step_count = attn.shape[0], attn.shape[1]
    attn = attn.reshape(row_count * step_count, width)
    def weighted(hidden):
        both = jnp.concatenate([hidden, other_core(hidden)], axis=0)
        both = both.reshape(scale.shape[0], -1, hidden.shape[1]).astype(jnp.float32) * scale / seqs
        both = both.astype(jnp.bfloat16).reshape(CORES * tokens, -1)
        return lax.optimization_barrier(both)

    own_factor = weighted(hidden_in)
    loads, _ = lax.optimization_barrier((attn, own_factor))
    loads = loads[None]
    for bit in (1, 2):
        got = send(loads, lambda x, zl, c, y, zh, bit=bit: (x, zl ^ bit, c, y, zh))
        upper = (zl & bit) != 0
        loads = jnp.concatenate(
            [jnp.where(upper, got, loads), jnp.where(upper, loads, got)], axis=0
        )

    late, loads = lax.optimization_barrier((hidden_in[:, SPANS[0][1] :], loads))
    far_late = send(late, lambda x, zl, c, y, zh: (x, zl, c, y, 1 - zh))

    near_attn = loads[:, : attn.shape[0]].reshape(1, -1, width)
    near_attn = [near_attn] + [
        send(near_attn, lambda x, zl, c, y, zh, s=s: (x ^ s, zl, c, y, zh)) for s in (1, 2, 3)
    ]

    def product(factor):
        out = lax.dot_general(
            every_grad, factor, (((1,), (0,)), ((), ())), preferred_element_type=jnp.float32
        )
        return out.astype(jnp.bfloat16).reshape(NY, 2 * rows, -1)

    def to_x(tiles):
        got = []
        for s in range(NX):
            tile = lax.dynamic_index_in_dim(tiles, (x + s) % NX, 0, keepdims=False)
            if s:
                tile = send(tile, lambda x, zl, c, y, zh, s=s: ((x + s) % NX, zl, c, y, zh))
            got.append(tile)
        return got

    def added(tiles):
        return sum(tile.astype(jnp.float32) for tile in tiles).reshape(2, rows, -1)

    tiles = product(own_factor)
    far_soon, near_attn, _ = lax.optimization_barrier((weighted(far_soon), near_attn, tiles))
    own = to_x(tiles)
    soon = to_x(product(far_soon))
    far_late, soon = lax.optimization_barrier((far_late, soon))
    tiles = product(weighted(far_late))
    far_sums = [added(soon), added(to_x(tiles))]
    own_sum = added(own)

    near_attn = jnp.concatenate(near_attn)
    got = other_core(near_attn)
    every_attn = jnp.stack(
        [jnp.where(core == 0, near_attn, got), jnp.where(core == 0, got, near_attn)], axis=1
    )
    every_attn = lax.optimization_barrier(every_attn.reshape(-1, width))

    pieces = []
    for (at, size), far in zip(SPANS, far_sums, strict=True):
        own = own_sum[:, :, at : at + size]
        blocks = jnp.stack([jnp.where(zh == 0, own, far), jnp.where(zh == 0, far, own)])
        low = zl % 2
        keep = lax.dynamic_index_in_dim(blocks, low, 1, keepdims=False)
        give = lax.dynamic_index_in_dim(blocks, 1 - low, 1, keepdims=False)
        give = give.astype(jnp.bfloat16)
        keep = keep + send(give, lambda x, zl, c, y, zh: (x, zl ^ 1, c, y, zh)).astype(jnp.float32)
        piece = None
        for s in range(2):
            block = lax.dynamic_index_in_dim(keep, (zl // 2) ^ s, 0, keepdims=False)
            block = send(
                block.astype(jnp.bfloat16),
                lambda x, zl, c, y, zh, s=s: (x, 2 * zh + zl % 2, c, y, (zl // 2) ^ s),
            ).astype(jnp.float32)
            piece = block if piece is None else piece + block
        pieces.append(piece)
    gradient = jnp.concatenate(pieces, axis=1)

    new_m = beta_one * adam_m + (1.0 - beta_one) * gradient
    new_v = beta_two * adam_v + (1.0 - beta_two) * gradient * gradient
    correct_one = 1.0 - beta_one**OPT_STEP
    correct_two = 1.0 - beta_two**OPT_STEP
    update = new_m / correct_one / (jnp.sqrt(new_v / correct_two) + adam_eps)
    new_weight = (
        weight.astype(jnp.float32) * (1.0 - learn_rate * decay_rate) - learn_rate * update
    ).astype(jnp.bfloat16)

    partial_out = lax.dot_general(
        new_weight, every_attn, (((1,), (1,)), ((), ())), preferred_element_type=jnp.float32
    ).astype(jnp.bfloat16)
    span = partial_out.shape[1] // NY
    summed = None
    for s in range(NY):
        block = lax.dynamic_slice_in_dim(partial_out, (x ^ y ^ s) * span, span, 1)
        block = send(block, lambda x, zl, c, y, zh, s=s: (y ^ s, zl, c, x, zh)).astype(jnp.float32)
        summed = block if summed is None else summed + block
    summed = summed.astype(jnp.bfloat16).reshape(2, rows // 2, CORES, ZL, -1)
    summed = summed.transpose(3, 2, 1, 0, 4).reshape(ZL * CORES, 1, rows // 2, -1)
    low = (zl < ZL // 2)
    none = jnp.zeros_like(summed)
    summed = jnp.concatenate(
        [jnp.where(low, summed, none), jnp.where(low, none, summed)], axis=1
    ).reshape(ZL * CORES * ZH, rows // 2, -1)
    in_column = [
        [flat(x, zl, c, y, zh) for zl in range(ZL) for c in range(CORES) for zh in range(ZH)]
        for x in range(NX)
        for y in range(NY)
    ]
    got = lax.all_to_all(
        summed, ("fsdp", "tp"), 0, 0, axis_index_groups=in_column, tiled=True
    )
    got = got.reshape(2, 4, ZH, rows // 2, 2, row_count * step_count)
    got = lax.dynamic_index_in_dim(got, zh, 0, keepdims=False).astype(jnp.float32)
    layer_out = (got[:, 0] + got[:, 1]).transpose(3, 0, 2, 1)
    layer_out = layer_out.reshape(row_count, step_count, width)
    return (new_weight, new_m, new_v, layer_out)


def solution(mesh):
    in_specs = (
        P("fsdp", "tp"),
        P("fsdp", "tp"),
        P("fsdp"),
        P(),
        P("fsdp", "tp"),
        P("fsdp", "tp"),
        P("fsdp", "tp"),
        P("fsdp", None, "tp"),
        P("fsdp", None, "tp"),
        P("fsdp", None, "tp"),
        P("fsdp", "tp", None, None),
        P("fsdp", "tp", None, None),
        P("fsdp"),
    )
    out_specs = (P("fsdp", "tp"), P("fsdp", "tp"), P("fsdp", "tp"), P("fsdp", None, "tp"))
    return jax.shard_map(
        per_device, mesh=mesh, in_specs=in_specs, out_specs=out_specs, check_vma=False
    )
```

```python
import math

import jax
import jax.numpy as jnp
from jax import lax
from jax.sharding import PartitionSpec as P

GSIZE = 8
OPT_STEP = 10

beta_one = 0.9
beta_two = 0.95
adam_eps = 1e-08
learn_rate = 0.002
decay_rate = 0.1
std_floor = 0.75

NX, ZL, CORES, NY, ZH = 4, 4, 2, 4, 2
SPANS = ((0, 384), (384, 256))


def send(value, dest):
    pairs = []
    for x in range(NX):
        for zl in range(ZL):
            for c in range(CORES):
                for y in range(NY):
                    for zh in range(ZH):
                        to = dest(x, zl, c, y, zh)
                        pairs.append((flat(x, zl, c, y, zh), flat(*to)))
    return lax.ppermute(value, ("fsdp", "tp"), pairs)


def flat(x, zl, c, y, zh):
    return ((x * ZL + zl) * CORES + c) * (NY * ZH) + y * ZH + zh


def other_core(value):
    return send(value, lambda x, zl, c, y, zh: (x, zl, 1 - c, y, zh))


def attend_local(query_in, key_new, value_new, key_cache, value_cache, lengths):
    row_count = query_in.shape[0]
    step_count = query_in.shape[1]
    kv_heads = key_cache.shape[1]
    cache_size = key_cache.shape[2]
    head_dim = key_cache.shape[3]
    group_size = query_in.shape[2] // (kv_heads * head_dim)
    scaling = 1.0 / math.sqrt(head_dim)
    query_heads = query_in.reshape(row_count, step_count, kv_heads, group_size, head_dim)
    fresh_keys = key_new.reshape(row_count, step_count, kv_heads, head_dim)
    fresh_values = value_new.reshape(row_count, step_count, kv_heads, head_dim)
    cache_score = (
        jnp.einsum("rsKgd,rKcd->rKgsc", query_heads, key_cache, preferred_element_type=jnp.float32)
        * scaling
    )
    fresh_score = (
        jnp.einsum("rsKgd,rtKd->rKgst", query_heads, fresh_keys, preferred_element_type=jnp.float32)
        * scaling
    )
    cache_mask = jnp.arange(cache_size, dtype=jnp.int32)[None, :] < lengths[:, None]
    step_index = jnp.arange(step_count, dtype=jnp.int32)
    fresh_mask = step_index[None, :] <= step_index[:, None]
    cache_score = jnp.where(cache_mask[:, None, None, None, :], cache_score, -jnp.inf)
    fresh_score = jnp.where(fresh_mask, fresh_score, -jnp.inf)
    peak_score = jnp.maximum(
        jnp.max(cache_score, axis=-1, keepdims=True), jnp.max(fresh_score, axis=-1, keepdims=True)
    )
    cache_exp = jnp.exp(cache_score - peak_score)
    fresh_exp = jnp.exp(fresh_score - peak_score)
    total_exp = jnp.sum(cache_exp, axis=-1, keepdims=True) + jnp.sum(
        fresh_exp, axis=-1, keepdims=True
    )
    cache_prob = (cache_exp / total_exp).astype(jnp.bfloat16)
    fresh_prob = (fresh_exp / total_exp).astype(jnp.bfloat16)
    mixed = jnp.einsum(
        "rKgsc,rKcd->rsKgd", cache_prob, value_cache, preferred_element_type=jnp.float32
    )
    mixed = mixed + jnp.einsum(
        "rKgst,rtKd->rsKgd", fresh_prob, fresh_values, preferred_element_type=jnp.float32
    )
    return mixed.reshape(row_count, step_count, kv_heads * group_size * head_dim).astype(
        jnp.bfloat16
    )


def chip_sequences(rewards, every_reward, group_ids, position, core):
    seq_dev = rewards.shape[0]
    seqs = seq_dev * lax.axis_size("fsdp")
    group_count = seqs // GSIZE
    labels = jnp.arange(group_count, dtype=jnp.int32)
    member = (group_ids[:, None] == labels[None, :]).astype(jnp.float32)
    group_mean = jnp.sum(member * every_reward[:, None], axis=0) / GSIZE
    spread = every_reward - jnp.sum(member * group_mean[None, :], axis=1)
    group_var = jnp.sum(member * (spread * spread)[:, None], axis=0) / (GSIZE - 1)
    own_std = jnp.sqrt(jnp.sum(member * group_var[None, :], axis=1))
    advantage = spread / jnp.maximum(own_std, std_floor)
    mine = lax.dynamic_slice_in_dim(advantage, position * seq_dev, seq_dev)
    theirs = lax.dynamic_slice_in_dim(advantage, (position + 1 - 2 * core) * seq_dev, seq_dev)
    return mine, theirs


def per_device(
    hidden_in,
    out_grad,
    rewards,
    group_ids,
    weight,
    adam_m,
    adam_v,
    given_queries,
    given_keys,
    given_values,
    stored_keys,
    stored_values,
    cache_fill_length,
):
    position = lax.axis_index("fsdp")
    tp_at = lax.axis_index("tp")
    x, zl, core = position // (ZL * CORES), (position // CORES) % ZL, position % CORES
    y, zh = tp_at // ZH, tp_at % ZH
    tokens, width = hidden_in.shape
    rows = weight.shape[0]
    seqs = rewards.shape[0] * lax.axis_size("fsdp")

    turned = out_grad.T.reshape(2, CORES, rows, tokens)
    keep = lax.dynamic_index_in_dim(turned, core, 1, keepdims=False)
    give = lax.dynamic_index_in_dim(turned, 1 - core, 1, keepdims=False)
    near = jnp.concatenate([keep, other_core(give)], axis=2).reshape(2 * rows, CORES * tokens)
    same_zh = [[y * ZH + zh for y in range(NY)] for zh in range(ZH)]
    every_grad = lax.all_gather(near, "tp", axis=0, tiled=True, axis_index_groups=same_zh)

    far_soon = send(hidden_in[:, : SPANS[0][1]], lambda x, zl, c, y, zh: (x, zl, c, y, 1 - zh))

    spot = jnp.zeros((1, seqs), jnp.float32)
    spot = lax.dynamic_update_slice(spot, rewards[None, :], (0, position * rewards.shape[0]))
    spot = spot + sum(
        send(spot, lambda x, zl, c, y, zh, s=s: (x, zl ^ s, c, y, zh)) for s in (1, 2, 3)
    )
    spot = spot + sum(
        send(spot, lambda x, zl, c, y, zh, s=s: (x ^ s, zl, c, y, zh)) for s in (1, 2, 3)
    )
    spot = spot + other_core(spot)
    mine, theirs = chip_sequences(rewards, spot[0], group_ids, position, core)
    scale = jnp.concatenate([mine, theirs])[:, None, None]

    attn = attend_local(
        given_queries, given_keys, given_values, stored_keys, stored_values, cache_fill_length
    )
    row_count, step_count = attn.shape[0], attn.shape[1]
    attn = attn.reshape(row_count * step_count, width)
    def weighted(hidden):
        both = jnp.concatenate([hidden, other_core(hidden)], axis=0)
        both = both.reshape(scale.shape[0], -1, hidden.shape[1]).astype(jnp.float32) * scale / seqs
        both = both.astype(jnp.bfloat16).reshape(CORES * tokens, -1)
        return lax.optimization_barrier(both)

    own_factor = weighted(hidden_in)
    loads, _ = lax.optimization_barrier((attn, own_factor))
    loads = loads[None]
    for bit in (1, 2):
        got = send(loads, lambda x, zl, c, y, zh, bit=bit: (x, zl ^ bit, c, y, zh))
        upper = (zl & bit) != 0
        loads = jnp.concatenate(
            [jnp.where(upper, got, loads), jnp.where(upper, loads, got)], axis=0
        )

    late, loads = lax.optimization_barrier((hidden_in[:, SPANS[0][1] :], loads))
    far_late = send(late, lambda x, zl, c, y, zh: (x, zl, c, y, 1 - zh))

    near_attn = loads[:, : attn.shape[0]].reshape(1, -1, width)
    near_attn = [near_attn] + [
        send(near_attn, lambda x, zl, c, y, zh, s=s: (x ^ s, zl, c, y, zh)) for s in (1, 2, 3)
    ]

    def product(factor):
        out = lax.dot_general(
            every_grad, factor, (((1,), (0,)), ((), ())), preferred_element_type=jnp.float32
        )
        return out.astype(jnp.bfloat16).reshape(NY, 2 * rows, -1)

    def to_x(tiles):
        got = []
        for s in range(NX):
            tile = lax.dynamic_index_in_dim(tiles, (x + s) % NX, 0, keepdims=False)
            if s:
                tile = send(tile, lambda x, zl, c, y, zh, s=s: ((x + s) % NX, zl, c, y, zh))
            got.append(tile)
        return got

    def added(tiles):
        return sum(tile.astype(jnp.float32) for tile in tiles).reshape(2, rows, -1)

    tiles = product(own_factor)
    far_soon, near_attn, _ = lax.optimization_barrier((weighted(far_soon), near_attn, tiles))
    own = to_x(tiles)
    soon = to_x(product(far_soon))
    far_late, soon = lax.optimization_barrier((far_late, soon))
    tiles = product(weighted(far_late))
    far_sums = [added(soon), added(to_x(tiles))]
    own_sum = added(own)

    near_attn, _ = lax.optimization_barrier((jnp.concatenate(near_attn), tiles))
    got = other_core(near_attn)
    every_attn = jnp.stack(
        [jnp.where(core == 0, near_attn, got), jnp.where(core == 0, got, near_attn)], axis=1
    )
    every_attn = lax.optimization_barrier(every_attn.reshape(-1, width))

    pieces = []
    for (at, size), far in zip(SPANS, far_sums, strict=True):
        own = own_sum[:, :, at : at + size]
        blocks = jnp.stack([jnp.where(zh == 0, own, far), jnp.where(zh == 0, far, own)])
        low = zl % 2
        keep = lax.dynamic_index_in_dim(blocks, low, 1, keepdims=False)
        give = lax.dynamic_index_in_dim(blocks, 1 - low, 1, keepdims=False)
        give = give.astype(jnp.bfloat16)
        keep = keep + send(give, lambda x, zl, c, y, zh: (x, zl ^ 1, c, y, zh)).astype(jnp.float32)
        piece = None
        for s in range(2):
            block = lax.dynamic_index_in_dim(keep, (zl // 2) ^ s, 0, keepdims=False)
            block = send(
                block.astype(jnp.bfloat16),
                lambda x, zl, c, y, zh, s=s: (x, 2 * zh + zl % 2, c, y, (zl // 2) ^ s),
            ).astype(jnp.float32)
            piece = block if piece is None else piece + block
        pieces.append(piece)
    gradient = jnp.concatenate(pieces, axis=1)

    new_m = beta_one * adam_m + (1.0 - beta_one) * gradient
    new_v = beta_two * adam_v + (1.0 - beta_two) * gradient * gradient
    correct_one = 1.0 - beta_one**OPT_STEP
    correct_two = 1.0 - beta_two**OPT_STEP
    update = new_m / correct_one / (jnp.sqrt(new_v / correct_two) + adam_eps)
    new_weight = (
        weight.astype(jnp.float32) * (1.0 - learn_rate * decay_rate) - learn_rate * update
    ).astype(jnp.bfloat16)

    partial_out = lax.dot_general(
        new_weight, every_attn, (((1,), (1,)), ((), ())), preferred_element_type=jnp.float32
    ).astype(jnp.bfloat16)
    span = partial_out.shape[1] // NY
    summed = None
    for s in range(NY):
        block = lax.dynamic_slice_in_dim(partial_out, (x ^ y ^ s) * span, span, 1)
        block = send(block, lambda x, zl, c, y, zh, s=s: (y ^ s, zl, c, x, zh)).astype(jnp.float32)
        summed = block if summed is None else summed + block
    summed = summed.astype(jnp.bfloat16).reshape(2, rows // 2, CORES, ZL, -1)
    summed = summed.transpose(3, 2, 1, 0, 4).reshape(ZL * CORES, 1, rows // 2, -1)
    low = (zl < ZL // 2)
    none = jnp.zeros_like(summed)
    summed = jnp.concatenate(
        [jnp.where(low, summed, none), jnp.where(low, none, summed)], axis=1
    ).reshape(ZL * CORES * ZH, rows // 2, -1)
    in_column = [
        [flat(x, zl, c, y, zh) for zl in range(ZL) for c in range(CORES) for zh in range(ZH)]
        for x in range(NX)
        for y in range(NY)
    ]
    got = lax.all_to_all(
        summed, ("fsdp", "tp"), 0, 0, axis_index_groups=in_column, tiled=True
    )
    got = got.reshape(2, 4, ZH, rows // 2, 2, row_count * step_count)
    got = lax.dynamic_index_in_dim(got, zh, 0, keepdims=False).astype(jnp.float32)
    layer_out = (got[:, 0] + got[:, 1]).transpose(3, 0, 2, 1)
    layer_out = layer_out.reshape(row_count, step_count, width)
    return (new_weight, new_m, new_v, layer_out)


def solution(mesh):
    in_specs = (
        P("fsdp", "tp"),
        P("fsdp", "tp"),
        P("fsdp"),
        P(),
        P("fsdp", "tp"),
        P("fsdp", "tp"),
        P("fsdp", "tp"),
        P("fsdp", None, "tp"),
        P("fsdp", None, "tp"),
        P("fsdp", None, "tp"),
        P("fsdp", "tp", None, None),
        P("fsdp", "tp", None, None),
        P("fsdp"),
    )
    out_specs = (P("fsdp", "tp"), P("fsdp", "tp"), P("fsdp", "tp"), P("fsdp", None, "tp"))
    return jax.shard_map(
        per_device, mesh=mesh, in_specs=in_specs, out_specs=out_specs, check_vma=False
    )
```
